512 devices in a mesh: ta: 4 (over z_hi), ha: 8 (over y, core), wa: 16 (over z_lo, x).
Axes of the slice: x: 4, y: 4, z: 16 (z_hi: 4, z_lo: 4; z = z_hi * 4 + z_lo), core: 2. Of those that a mesh axis runs over, the one named last changes fastest.
Arguments:
- queries: bfloat16 [24, 64, 128, 128], P('ta', 'ha', 'wa'), may hold values from -30 to 30
- keys: bfloat16 [24, 64, 128, 128], P('ta', 'ha', 'wa'), may hold values from -30 to 30
- values: bfloat16 [24, 64, 128, 128], P('ta', 'ha', 'wa'), may hold values from -6 to 6
- out_grad: bfloat16 [24, 64, 128, 128], P('ta', 'ha', 'wa'), may hold values from -6 to 6
- window_extent: int32 [4, 8, 16, 3], replicated, may hold values from 0 to 1, as said below
- pair_table: int32 [1, 27], replicated, may hold values from 0 to 1, as said below
Outputs:
- attended: bfloat16 [24, 64, 128, 128], P('ta', 'ha', 'wa')
- query_grad: bfloat16 [24, 64, 128, 128], P('ta', 'ha', 'wa')
- key_grad: bfloat16 [24, 64, 128, 128], P('ta', 'ha', 'wa')
- value_grad: bfloat16 [24, 64, 128, 128], P('ta', 'ha', 'wa')
The draws below stay inside these ranges and needn't reach their ends.
Inputs may be any that keep to these rules, and one draw needn't show every extreme that they name: `window_extent`: at least one tile has 1 on all three axes and at least one has 0 on all three. `pair_table`: entry 13 (the tile itself) and the face offsets 4, 10, 12, 14, 16, 22 are 1 for every head.
All inputs are finite; a program needn't handle non-finite values.
Results may differ from the reference program's by a relative error of at most 0.0093.
Values may be sent and summed in bfloat16 or wider, within the bound.
No kernel may reach another device: no remote copies, remote signals or barrier semaphores. Data moves between devices by JAX's collectives and lax.ppermute only.
A program may use at most 64 MiB of HBM per device.

```python
import jax
import jax.numpy as jnp
import numpy as np
from jax import lax

HD = 128
HEADS = 1
TT = 6
TH = 8
TW = 8
TILES_T = 4
TILES_H = 8
TILES_W = 16
NT = 24
NH = 64
NW = 128


def draw_queries(key, part):
    full_shape = (NT, NH, NW, HEADS * HD)
    key = jax.random.fold_in(key, 1)
    result = jax.random.normal(key, full_shape, jnp.float32)
    return jnp.clip(result, -30.0, 30.0).astype(jnp.bfloat16)


def draw_keys(key, part):
    full_shape = (NT, NH, NW, HEADS * HD)
    key = jax.random.fold_in(key, 2)
    result = jax.random.normal(key, full_shape, jnp.float32)
    return jnp.clip(result, -30.0, 30.0).astype(jnp.bfloat16)


def draw_window_extent(key, part):
    key = jax.random.fold_in(key, 3)
    tile_total = TILES_T * TILES_H * TILES_W
    loose_bits = (jax.random.randint(jax.random.fold_in(key, 0), (tile_total, 3), 0, 4) >= 1).astype(jnp.int32)
    widest = jax.random.randint(jax.random.fold_in(key, 1), (), 0, tile_total)
    narrow = (widest + 1 + jax.random.randint(jax.random.fold_in(key, 2), (), 0, tile_total - 1)) % tile_total
    tile_index = jnp.arange(tile_total)[:, None]
    flat_ext = jnp.where(tile_index == widest, 1, jnp.where(tile_index == narrow, 0, loose_bits))
    return flat_ext.reshape(TILES_T, TILES_H, TILES_W, 3).astype(jnp.int32)


def draw_pair_table(key, part):
    key = jax.random.fold_in(key, 4)
    face_list = [4, 10, 12, 13, 14, 16, 22]
    other_list = jnp.asarray(np.array([entry for entry in range(27) if entry not in face_list], dtype=np.int32))
    random_bits = jax.random.randint(jax.random.fold_in(key, 0), (HEADS, 27), 0, 2)
    slots = jnp.arange(27)
    forced = jnp.any(slots[:, None] == jnp.asarray(np.array(face_list, dtype=np.int32))[None, :], axis=1)[None, :]
    dropped = other_list[jax.random.randint(jax.random.fold_in(key, 1), (HEADS,), 0, 20)]
    return jnp.where(forced, 1, jnp.where(slots[None, :] == dropped[:, None], 0, random_bits)).astype(jnp.int32)


def shard_levels(key, shape, cuts, least, high):
    factor_of = 1.0
    for dim, shards_of in cuts:
        heights = jax.random.uniform(jax.random.fold_in(jax.random.fold_in(key, 6), dim), (shards_of,), jnp.float32, least / len(cuts), high / len(cuts))
        factor_of = factor_of * jnp.repeat(jnp.exp(heights), shape[dim] // shards_of).reshape((-1,) + (1,) * (len(shape) - 1 - dim))
    return factor_of


def gaussian(stream_key, extent, deviation, bound, split=(), kind=jnp.bfloat16):
    factor_of = shard_levels(stream_key, extent, split, -0.22, 0.18) if split else 1.0
    values = jax.random.normal(stream_key, extent, jnp.float32) * deviation * factor_of
    return jnp.minimum(jnp.maximum(values, -bound), bound).astype(kind)


def setup_inputs(seed: int = 0) -> dict:
    key_of = jax.random.split(jax.random.key(seed), 7)
    return {
        "queries": draw_queries(jax.random.fold_in(key_of[6], 71), 0),
        "keys": draw_keys(jax.random.fold_in(key_of[6], 71), 0),
        "values": gaussian(key_of[2], (NT, NH, NW, HEADS * HD), 1.0, 6.0, ((0, 4), (1, 8), (2, 16))),
        "out_grad": gaussian(key_of[3], (NT, NH, NW, HEADS * HD), 1.0, 6.0, ((0, 4), (1, 8), (2, 16))),
        "window_extent": draw_window_extent(jax.random.fold_in(key_of[6], 71), 0),
        "pair_table": draw_pair_table(jax.random.fold_in(key_of[6], 71), 0),
    }


offset_table = np.array([[a - 1, b - 1, c - 1] for a in range(3) for b in range(3) for c in range(3)], dtype=np.int32)


def to_tile_grid(block):
    span_t, span_h, span_w, row_width = block.shape
    grid = block.reshape(span_t // TT, TT, span_h // TH, TH, span_w // TW, TW, row_width)
    return grid.transpose(0, 2, 4, 1, 3, 5, 6).reshape(span_t // TT, span_h // TH, span_w // TW, TT * TH * TW, row_width)


def from_tile_grid(tiled):
    grid_t, grid_h, grid_w, tile_rows, row_width = tiled.shape
    grid = tiled.reshape(grid_t, grid_h, grid_w, TT, TH, TW, row_width)
    return grid.transpose(0, 3, 1, 4, 2, 5, 6).reshape(grid_t * TT, grid_h * TH, grid_w * TW, row_width)


def pad_grid(tiled):
    return jnp.pad(tiled, ((1, 1), (1, 1), (1, 1)) + ((0, 0),) * (tiled.ndim - 3))


def window_of(padded, tile_index):
    tile_t = (tile_index // (TILES_H * TILES_W)).astype(jnp.int32)
    tile_h = ((tile_index // TILES_W) % TILES_H).astype(jnp.int32)
    tile_w = (tile_index % TILES_W).astype(jnp.int32)
    zero_start = jnp.zeros((), jnp.int32)
    starts = (tile_t, tile_h, tile_w) + (zero_start,) * (padded.ndim - 3)
    window = lax.dynamic_slice(padded, starts, (3, 3, 3) + padded.shape[3:])
    return window.reshape((27,) + padded.shape[3:])


def reference(queries, keys, values, out_grad, window_extent, pair_table):
    row_width = queries.shape[3]
    head_count = pair_table.shape[0]
    head_depth = row_width // head_count
    score_scale = head_depth ** -0.5
    tile_rows = TT * TH * TW
    tile_total = TILES_T * TILES_H * TILES_W
    distance = jnp.abs(jnp.asarray(offset_table))
    pair_kept = pair_table == 1
    reverse = pair_kept[:, ::-1]
    query_pad = pad_grid(to_tile_grid(queries))
    key_pad = pad_grid(to_tile_grid(keys))
    value_pad = pad_grid(to_tile_grid(values))
    grad_pad = pad_grid(to_tile_grid(out_grad))
    valid_pad = pad_grid(jnp.ones((TILES_T, TILES_H, TILES_W), jnp.float32))
    extent_pad = pad_grid(window_extent)

    def heads_of(rows_in):
        return rows_in.reshape(rows_in.shape[:-1] + (head_count, head_depth)).astype(jnp.float32)

    def query_tile(tile_index):
        own_query = heads_of(window_of(query_pad, tile_index)[13])
        own_grad = heads_of(window_of(grad_pad, tile_index)[13])
        key_near = heads_of(window_of(key_pad, tile_index).reshape(27 * tile_rows, row_width))
        value_near = heads_of(window_of(value_pad, tile_index).reshape(27 * tile_rows, row_width))
        valid_near = window_of(valid_pad, tile_index) > 0.5
        own_ext = window_of(extent_pad, tile_index)[13]
        near_ok = jnp.all(distance <= own_ext[None, :], axis=1) & valid_near
        allow_tile = pair_kept & near_ok[None, :]
        allow = jnp.broadcast_to(allow_tile[:, None, :, None], (head_count, tile_rows, 27, tile_rows)).reshape(head_count, tile_rows, 27 * tile_rows)
        scores = jnp.einsum('qhd,khd->hqk', own_query, key_near) * score_scale
        row_peak = jnp.max(jnp.where(allow, scores, -jnp.inf), axis=2, keepdims=True)
        row_total = jnp.sum(jnp.exp(jnp.where(allow, scores - row_peak, -jnp.inf)), axis=2, keepdims=True)
        log_norm = row_peak + jnp.log(row_total)
        chance = jnp.exp(jnp.where(allow, scores - log_norm, -jnp.inf))
        chance_bf = chance.astype(jnp.bfloat16)
        mixed = jnp.einsum('hqk,khd->qhd', chance_bf.astype(jnp.float32), value_near)
        delta_row = jnp.sum(own_grad * mixed, axis=2)
        grad_chance = jnp.einsum('qhd,khd->hqk', own_grad, value_near)
        grad_score = (chance * (grad_chance - delta_row.T[:, :, None]) * score_scale).astype(jnp.bfloat16)
        query_sum = jnp.einsum('hqk,khd->qhd', grad_score.astype(jnp.float32), key_near)
        return (mixed.reshape(tile_rows, row_width).astype(jnp.bfloat16),
                query_sum.reshape(tile_rows, row_width).astype(jnp.bfloat16),
                log_norm[:, :, 0].T, delta_row)

    tile_ids = jnp.arange(tile_total, dtype=jnp.int32)
    mixed_all, query_all, norm_all, delta_all = lax.map(query_tile, tile_ids)
    stat_shape = (TILES_T, TILES_H, TILES_W, tile_rows, head_count)
    norm_pad = pad_grid(norm_all.reshape(stat_shape))
    delta_pad = pad_grid(delta_all.reshape(stat_shape))

    def key_tile(tile_index):
        own_key = heads_of(window_of(key_pad, tile_index)[13])
        own_value = heads_of(window_of(value_pad, tile_index)[13])
        query_near = heads_of(window_of(query_pad, tile_index).reshape(27 * tile_rows, row_width))
        grad_near = heads_of(window_of(grad_pad, tile_index).reshape(27 * tile_rows, row_width))
        norm_near = window_of(norm_pad, tile_index).reshape(27 * tile_rows, head_count)
        delta_near = window_of(delta_pad, tile_index).reshape(27 * tile_rows, head_count)
        valid_near = window_of(valid_pad, tile_index) > 0.5
        ext_near = window_of(extent_pad, tile_index)
        near_ok = jnp.all(distance <= ext_near, axis=1) & valid_near
        allow_tile = reverse & near_ok[None, :]
        allow = jnp.broadcast_to(allow_tile[:, :, None, None], (head_count, 27, tile_rows, tile_rows)).reshape(head_count, 27 * tile_rows, tile_rows)
        scores = jnp.einsum('qhd,khd->hqk', query_near, own_key) * score_scale
        chance = jnp.exp(jnp.where(allow, scores - norm_near.T[:, :, None], -jnp.inf))
        chance_bf = chance.astype(jnp.bfloat16)
        grad_chance = jnp.einsum('qhd,khd->hqk', grad_near, own_value)
        grad_score = (chance * (grad_chance - delta_near.T[:, :, None]) * score_scale).astype(jnp.bfloat16)
        key_sum = jnp.einsum('hqk,qhd->khd', grad_score.astype(jnp.float32), query_near)
        value_sum = jnp.einsum('hqk,qhd->khd', chance_bf.astype(jnp.float32), grad_near)
        return (key_sum.reshape(tile_rows, row_width).astype(jnp.bfloat16),
                value_sum.reshape(tile_rows, row_width).astype(jnp.bfloat16))

    key_all, value_all = lax.map(key_tile, tile_ids)
    grid_shape = (TILES_T, TILES_H, TILES_W, tile_rows, row_width)
    attended = from_tile_grid(mixed_all.reshape(grid_shape))
    query_grad = from_tile_grid(query_all.reshape(grid_shape))
    key_grad = from_tile_grid(key_all.reshape(grid_shape))
    value_grad = from_tile_grid(value_all.reshape(grid_shape))
    return (attended, query_grad, key_grad, value_grad)
```

```python
import functools

import jax
import jax.numpy as jnp
import numpy as np
from jax import lax
from jax.experimental import pallas as pl
from jax.experimental.pallas import tpu as pltpu
from jax.sharding import PartitionSpec as P

ROWS = 384
DEPTH = 128
SCALE = DEPTH ** -0.5
LOG2E = 1.4426950408889634
SCALE2 = SCALE * LOG2E
VMEM_LIMIT = 40 * 1024 * 1024

OFFSETS = np.array(
    [[a - 1, b - 1, c - 1] for a in range(3) for b in range(3) for c in range(3)], dtype=np.int32
)
NT_DIMS = (((1,), (1,)), ((), ()))
NN_DIMS = (((1,), (0,)), ((), ()))


def swap(value, axis):
    size = lax.axis_size(axis)
    results = []
    for first in (0, 1):
        pairs = []
        for i in range(first, size - 1, 2):
            pairs += [(i, i + 1), (i + 1, i)]
        results.append(lax.ppermute(value, axis, pairs))
    return results


def allowed_slots(window_extent, pair_table):
    counts = window_extent.shape[:3]
    coords = (lax.axis_index("ta"), lax.axis_index("ha"), lax.axis_index("wa"))
    distance = jnp.abs(jnp.asarray(OFFSETS))
    inside = jnp.ones((27,), jnp.bool_)
    for axis in range(3):
        position = coords[axis] + jnp.asarray(OFFSETS[:, axis])
        inside = inside & (position >= 0) & (position < counts[axis])
    padded = jnp.pad(window_extent, ((1, 1), (1, 1), (1, 1), (0, 0)))
    near = lax.dynamic_slice(padded, coords + (jnp.int32(0),), (3, 3, 3, 3)).reshape(27, 3)
    kept = pair_table[0] == 1
    as_query = kept & inside & jnp.all(distance <= near[13][None, :], axis=1)
    as_key = kept[::-1] & inside & jnp.all(distance <= near, axis=1)
    both = jnp.stack([as_query, as_key]).astype(jnp.int32)
    place = jnp.zeros((3, 3, 3), jnp.int32)
    for axis, weight in ((0, 9), (1, 3), (2, 1)):
        sign = 1 - 2 * (coords[axis] % 2)
        shape = [1, 1, 1]
        shape[axis] = 3
        step = jnp.asarray(np.array([0, 1, -1], dtype=np.int32)) * sign + 1
        place = place + weight * step.reshape(shape)
    place = place.reshape(27)
    hot = place[:, None] == jnp.arange(27, dtype=jnp.int32)[None, :]
    slots = jnp.sum(jnp.where(hot[None], both[:, None, :], 0), axis=2).reshape(2, 3, 3, 3)
    plane = slots[:, 0].reshape(2, 9)
    rest = slots[:, 1:].transpose(0, 2, 3, 1).reshape(2, 18)
    return plane[0], rest[0], plane[1], rest[1]


def each_block(allow_ref, stacks, count, step):
    for part in range(3):
        def body(i, carry, part=part):
            @pl.when(allow_ref[part * count + i] == 1)
            def _():
                step(stacks[part], i)
            return carry
        lax.fori_loop(0, count, body, 0)


def forward_step(q_ref, peak, total, acc, stack, i):
    scores = lax.dot_general(q_ref[...], stack[i, 0], NT_DIMS, preferred_element_type=jnp.float32)
    old = peak[:, :1]
    new = jnp.maximum(old, jnp.max(scores, axis=1, keepdims=True))
    chance = jnp.exp2((scores - new) * SCALE2)
    shrink = jnp.exp2((old - new) * SCALE2)
    total[:, :1] = total[:, :1] * shrink + jnp.sum(chance, axis=1, keepdims=True)
    peak[:, :1] = new
    mixed = lax.dot_general(
        chance.astype(jnp.bfloat16), stack[i, 1], NN_DIMS, preferred_element_type=jnp.float32
    )
    acc[...] = acc[...] * shrink + mixed


def forward_first(allow_ref, q_ref, s0, s1, s2, peak, total, acc):
    peak[...] = jnp.full(peak.shape, -1e30, jnp.float32)
    total[...] = jnp.zeros(total.shape, jnp.float32)
    acc[...] = jnp.zeros(acc.shape, jnp.float32)
    each_block(allow_ref, (s0, s1, s2), 3, functools.partial(forward_step, q_ref, peak, total, acc))


def forward_last(
    allow_ref, q_ref, g_ref, s0, s1, s2, peak_in, total_in, acc_in,
    out_ref, rows_ref, cols_ref, peak, total, acc,
):
    peak[...] = peak_in[...]
    total[...] = total_in[...]
    acc[...] = acc_in[...]
    each_block(allow_ref, (s0, s1, s2), 6, functools.partial(forward_step, q_ref, peak, total, acc))
    mixed = acc[...] / total[:, :1]
    out_ref[...] = mixed.astype(out_ref.dtype)
    delta = jnp.sum(mixed * g_ref[...].astype(jnp.float32), axis=1, keepdims=True)
    norm = peak[:, :1] * SCALE2 + jnp.log2(total[:, :1])
    lane = lax.broadcasted_iota(jnp.int32, (ROWS, DEPTH), 1)
    cols = jnp.where(lane == 0, norm, delta)
    cols_ref[...] = cols
    rows_ref[...] = cols.T[:8]


def query_side(
    allow0, allow1, q_ref, g_ref, cols_ref, a0, a1, a2, b0, b1, b2, out_ref, acc
):
    acc[...] = jnp.zeros(acc.shape, jnp.float32)

    def step(stack, i):
        key, value = stack[i, 0], stack[i, 1]
        scores = lax.dot_general(q_ref[...], key, NT_DIMS, preferred_element_type=jnp.float32)
        chance = jnp.exp2(scores * SCALE2 - cols_ref[:, :1])
        grad_chance = lax.dot_general(g_ref[...], value, NT_DIMS, preferred_element_type=jnp.float32)
        grad_score = (chance * (grad_chance - cols_ref[:, 1:2]) * SCALE).astype(jnp.bfloat16)
        acc[...] += lax.dot_general(grad_score, key, NN_DIMS, preferred_element_type=jnp.float32)

    each_block(allow0, (a0, a1, a2), 3, step)
    each_block(allow1, (b0, b1, b2), 6, step)
    out_ref[...] = acc[...].astype(out_ref.dtype)


def key_side(count, finish, allow_ref, k_ref, v_ref, s0, s1, s2, r0, r1, r2, *rest):
    if finish:
        key_in, value_in, key_out, value_out, key_acc, value_acc = rest
        key_acc[...] = key_in[...]
        value_acc[...] = value_in[...]
    else:
        key_acc, value_acc = rest
        key_acc[...] = jnp.zeros(key_acc.shape, jnp.float32)
        value_acc[...] = jnp.zeros(value_acc.shape, jnp.float32)

    def step(refs, i):
        stack, rows = refs
        query, grad = stack[i, 0], stack[i, 1]
        stat = rows[i]
        scores = lax.dot_general(k_ref[...], query, NT_DIMS, preferred_element_type=jnp.float32)
        chance = jnp.exp2(scores * SCALE2 - stat[0:1, :])
        grad_chance = lax.dot_general(v_ref[...], grad, NT_DIMS, preferred_element_type=jnp.float32)
        grad_score = (chance * (grad_chance - stat[1:2, :]) * SCALE).astype(jnp.bfloat16)
        key_acc[...] += lax.dot_general(grad_score, query, NN_DIMS, preferred_element_type=jnp.float32)
        value_acc[...] += lax.dot_general(
            chance.astype(jnp.bfloat16), grad, NN_DIMS, preferred_element_type=jnp.float32
        )

    each_block(allow_ref, ((s0, r0), (s1, r1), (s2, r2)), count, step)
    if finish:
        key_out[...] = key_acc[...].astype(key_out.dtype)
        value_out[...] = value_acc[...].astype(value_out.dtype)


def call(kernel, name, in_smem, out_shape, scratch=(), blocks=9):
    smem = pl.BlockSpec(memory_space=pltpu.SMEM)
    vmem = pl.BlockSpec(memory_space=pltpu.VMEM)
    area = blocks * ROWS * ROWS

    def run(*operands):
        return pl.pallas_call(
            kernel,
            out_shape=out_shape,
            in_specs=[smem if i < in_smem else vmem for i in range(len(operands))],
            out_specs=jax.tree.map(lambda _: vmem, out_shape),
            scratch_shapes=list(scratch),
            compiler_params=pltpu.CompilerParams(vmem_limit_bytes=VMEM_LIMIT),
            cost_estimate=pl.CostEstimate(
                flops=area * DEPTH * 8, transcendentals=area, bytes_accessed=blocks * ROWS * DEPTH * 4
            ),
            name=name,
        )(*operands)

    return run


def halo_first(own):
    first = jnp.stack([own] + swap(own, "wa"))
    return [first] + swap(first, "ha")


def halo_rest(own):
    planes = jnp.stack(swap(own, "ta"))
    row = jnp.concatenate([planes] + swap(planes, "wa"))
    return [row] + swap(row, "ha")


def on_device(queries, keys, values, out_grad, window_extent, pair_table):
    out_block = queries.shape
    q, k, v, g = (x.reshape(ROWS, DEPTH) for x in (queries, keys, values, out_grad))
    query0, query1, key0, key1 = allowed_slots(window_extent, pair_table)
    wide = jax.ShapeDtypeStruct((ROWS, DEPTH), jnp.float32)
    narrow = jax.ShapeDtypeStruct((ROWS, DEPTH), jnp.bfloat16)
    wide_scratch = pltpu.VMEM((ROWS, DEPTH), jnp.float32)
    rows_shape = jax.ShapeDtypeStruct((8, ROWS), jnp.float32)

    kv = jnp.stack([k, v])
    qg = jnp.stack([q, g])
    kv0 = halo_first(kv)
    kv1 = halo_rest(kv)
    qg0 = halo_first(qg)
    qg1 = halo_rest(qg)

    state = call(forward_first, "forward_first", 1, (wide, wide, wide))(query0, q, *kv0)
    attended, rows, cols = call(
        forward_last, "forward_last", 1, (narrow, rows_shape, wide), [wide_scratch] * 3, 18
    )(query1, q, g, *kv1, *state)
    rows0 = halo_first(rows)
    rows1 = halo_rest(rows)
    query_grad = call(query_side, "query_side", 2, narrow, [wide_scratch], 27)(
        query0, query1, q, g, cols, *kv0, *kv1
    )
    partial = call(functools.partial(key_side, 3, False), "key_first", 1, (wide, wide))(
        key0, k, v, *qg0, *rows0
    )
    key_grad, value_grad = call(
        functools.partial(key_side, 6, True), "key_last", 1, (narrow, narrow), [wide_scratch] * 2, 18
    )(key1, k, v, *qg1, *rows1, *partial)
    return tuple(x.reshape(out_block) for x in (attended, query_grad, key_grad, value_grad))


def solution(mesh):
    split = P("ta", "ha", "wa", None)
    return jax.shard_map(
        on_device,
        mesh=mesh,
        in_specs=(split, split, split, split, P(), P()),
        out_specs=(split, split, split, split),
        check_vma=False,
    )
```

```python
import math

import jax
import jax.numpy as jnp
import numpy as np
from jax import lax
from jax.experimental import pallas as pl
from jax.experimental.pallas import tpu as pltpu
from jax.sharding import PartitionSpec as P

ROWS = 384
DEPTH = 128
SCALE = DEPTH ** -0.5
LOG2E = 1.4426950408889634
SCALE2 = SCALE * LOG2E
PLACES = 27
STAT_ROWS = 32
BLOCK_ROWS = 2 * ROWS + STAT_ROWS
LINE_ROWS = 2 * BLOCK_ROWS + STAT_ROWS
FORWARD_GROUP = 6
BACKWARD_GROUP = 3
MASKED = 1e30
VMEM_LIMIT = 40 * 1024 * 1024

OFFSETS = np.array(
    [[a - 1, b - 1, c - 1] for a in range(3) for b in range(3) for c in range(3)], dtype=np.int32
)
NT_DIMS = (((1,), (1,)), ((), ()))
NN_DIMS = (((1,), (0,)), ((), ()))


def swap(value, axis):
    size = lax.axis_size(axis)
    results = []
    for first in (0, 1):
        pairs = []
        for i in range(first, size - 1, 2):
            pairs += [(i, i + 1), (i + 1, i)]
        results.append(lax.ppermute(value, axis, pairs))
    return results


def allowed_slots(window_extent, pair_table):
    counts = window_extent.shape[:3]
    coords = (lax.axis_index("ta"), lax.axis_index("ha"), lax.axis_index("wa"))
    distance = jnp.abs(jnp.asarray(OFFSETS))
    inside = jnp.ones((27,), jnp.bool_)
    for axis in range(3):
        position = coords[axis] + jnp.asarray(OFFSETS[:, axis])
        inside = inside & (position >= 0) & (position < counts[axis])
    padded = jnp.pad(window_extent, ((1, 1), (1, 1), (1, 1), (0, 0)))
    near = lax.dynamic_slice(padded, coords + (jnp.int32(0),), (3, 3, 3, 3)).reshape(27, 3)
    kept = pair_table[0] == 1
    as_query = kept & inside & jnp.all(distance <= near[13][None, :], axis=1)
    as_key = kept[::-1] & inside & jnp.all(distance <= near, axis=1)
    both = jnp.stack([as_query, as_key]).astype(jnp.int32)
    place = jnp.zeros((3, 3, 3), jnp.int32)
    for axis, weight in ((0, 9), (1, 3), (2, 1)):
        sign = 1 - 2 * (coords[axis] % 2)
        shape = [1, 1, 1]
        shape[axis] = 3
        step = jnp.asarray(np.array([0, 1, -1], dtype=np.int32)) * sign + 1
        place = place + weight * step.reshape(shape)
    place = place.reshape(27)
    hot = place[:, None] == jnp.arange(27, dtype=jnp.int32)[None, :]
    slots = jnp.sum(jnp.where(hot[None], both[:, None, :], 0), axis=2)
    slots = slots.reshape(2, 3, 9)
    plane = slots[:, 0]
    rest = slots[:, 1:].transpose(0, 2, 1).reshape(2, 18)
    return jnp.concatenate([plane, rest], axis=1).reshape(2 * PLACES)


def matmul(left, right, dims):
    return lax.dot_general(left, right, dims, preferred_element_type=jnp.float32)


def thirds(wide):
    return [wide[:, i * DEPTH : (i + 1) * DEPTH] for i in range(ROWS // DEPTH)]


def compact(flags, near, rest, kv):
    place = jnp.int32(0)
    first = 0
    for part, count in [(x, 3) for x in near] + [(x, 6) for x in rest]:

        def body(i, place, first=first, part=part):
            flag = flags[first + i]

            @pl.when(flag == 1)
            def _():
                kv[place] = part[i, :2]

            return place + flag

        place = lax.fori_loop(0, count, body, place)
        first += count
    return place


def each_group(number, size, step):
    def body(group, carry):
        blocks, biases = [], []
        for k in range(size):
            at = group * size + k
            blocks.append(jnp.minimum(at, number - 1))
            biases.append(jnp.where(at < number, 0.0, MASKED).astype(jnp.float32))
        step(blocks, biases)
        return carry

    lax.fori_loop(0, lax.div(number + size - 1, size), body, 0)


def forward(
    flags, q_ref, g_ref, n0, n1, n2, s0, s1, s2,
    out_ref, stat_ref, norm_ref, delta_ref, kv, peak, total, acc, stat,
):
    number = compact(flags, (n0, n1, n2), (s0, s1, s2), kv)
    peak[...] = jnp.full(peak.shape, -MASKED, jnp.float32)
    total[...] = jnp.zeros(total.shape, jnp.float32)
    acc[...] = jnp.zeros(acc.shape, jnp.float32)

    def step(blocks, biases):
        query = q_ref[...]
        scores = [matmul(query, kv[b, 0], NT_DIMS) for b in blocks]
        old = peak[...]
        best = old
        for score, bias in zip(scores, biases):
            a, b, c = thirds(score)
            best = jnp.maximum(best, jnp.maximum(jnp.maximum(a, b), c) - bias)
        new = jnp.broadcast_to(jnp.max(best, axis=1, keepdims=True), best.shape)
        peak[...] = new
        shrink = jnp.exp2((old - new) * SCALE2)
        norm = new * SCALE2
        whole = total[...] * shrink
        mixed = acc[...] * shrink
        for block, score, bias in zip(blocks, scores, biases):
            at = norm + bias
            a, b, c = (jnp.exp2(x * SCALE2 - at) for x in thirds(score))
            whole = whole + (a + b + c)
            chance = jnp.concatenate([x.astype(jnp.bfloat16) for x in (a, b, c)], axis=1)
            mixed = mixed + matmul(chance, kv[block, 1], NN_DIMS)
        total[...] = whole
        acc[...] = mixed

    each_group(number, FORWARD_GROUP, step)
    whole = jnp.sum(total[...], axis=1, keepdims=True)
    mixed = acc[...] / whole
    out_ref[...] = mixed.astype(out_ref.dtype)
    delta = jnp.sum(mixed * g_ref[...].astype(jnp.float32), axis=1, keepdims=True)
    norm = peak[:, :1] * SCALE2 + jnp.log2(whole)
    lane = lax.broadcasted_iota(jnp.int32, (ROWS, DEPTH), 1)
    both = jnp.where(lane == 0, norm, delta).T[:8]
    stat[...] = jnp.zeros(stat.shape, jnp.float32)
    for kind in range(2):
        left = both[kind : kind + 1]
        for part in range(3):
            rounded = left.astype(jnp.bfloat16).astype(jnp.float32)
            left = left - rounded
            for c, piece in enumerate(thirds(rounded)):
                row = 9 * kind + 3 * part + c
                stat[row : row + 1] = piece
    stat_ref[...] = stat[...].astype(stat_ref.dtype)
    norm_ref[...] = jnp.broadcast_to(norm - math.log2(SCALE), norm_ref.shape)
    delta_ref[...] = jnp.broadcast_to(delta, delta_ref.shape)


def query_side(
    flags, q_ref, g_ref, norm_ref, delta_ref, n0, n1, n2, s0, s1, s2, out_ref, kv, acc
):
    number = compact(flags, (n0, n1, n2), (s0, s1, s2), kv)
    acc[...] = jnp.zeros(acc.shape, jnp.float32)

    def step(blocks, biases):
        query, grad = q_ref[...], g_ref[...]
        norm, delta = norm_ref[...], delta_ref[...]
        scores = [matmul(query, kv[b, 0], NT_DIMS) for b in blocks]
        grad_chances = [matmul(grad, kv[b, 1], NT_DIMS) for b in blocks]
        sum_of = acc[...]
        for block, score, grad_chance, bias in zip(blocks, scores, grad_chances, biases):
            at = norm + bias
            parts = [
                (jnp.exp2(x * SCALE2 - at) * (y - delta)).astype(jnp.bfloat16)
                for x, y in zip(thirds(score), thirds(grad_chance))
            ]
            sum_of = sum_of + matmul(jnp.concatenate(parts, axis=1), kv[block, 0], NN_DIMS)
        acc[...] = sum_of

    each_group(number, BACKWARD_GROUP, step)
    out_ref[...] = acc[...].astype(out_ref.dtype)


def key_side(
    flags, k_ref, v_ref, n0, n1, n2, m0, m1, m2,
    key_out, value_out, qg, rows, key_acc, value_acc,
):
    place = jnp.int32(0)
    slots = [(n, m, w, None) for n, m in zip((n0, n1, n2), (m0, m1, m2)) for w in range(3)]
    slots += [(None, m, w, t) for m in (m0, m1, m2) for w in range(3) for t in range(2)]
    for at, (near, rest, w, t) in enumerate(slots):
        flag = flags[PLACES + at]

        @pl.when(flag == 1)
        def _(place=place, near=near, rest=rest, w=w, t=t):
            if t is None:
                first = 2 * BLOCK_ROWS
                qg[place] = near[w, 2:]
            else:
                first = BLOCK_ROWS * t + 2 * ROWS
                qg[place, 0] = rest[w, first - 2 * ROWS : first - ROWS]
                qg[place, 1] = rest[w, first - ROWS : first]
            stat = rest[w, first : first + STAT_ROWS].astype(jnp.float32)
            for kind in range(2):
                for c in range(3):
                    high, mid, low = (stat[r : r + 1] for r in range(9 * kind + c, 9 * kind + c + 9, 3))
                    rows[place, kind : kind + 1, c * DEPTH : (c + 1) * DEPTH] = high + (mid + low)

        place = place + flag
    number = place
    key_acc[...] = jnp.zeros(key_acc.shape, jnp.float32)
    value_acc[...] = jnp.zeros(value_acc.shape, jnp.float32)

    def step(blocks, biases):
        key, value = k_ref[...], v_ref[...]
        scores = [matmul(key, qg[b, 0], NT_DIMS) for b in blocks]
        grad_chances = [matmul(value, qg[b, 1], NT_DIMS) for b in blocks]
        key_sum, value_sum = key_acc[...], value_acc[...]
        for block, score, grad_chance, bias in zip(blocks, scores, grad_chances, biases):
            stat = rows[block]
            chance = jnp.exp2(score * SCALE2 - (stat[0:1, :] + bias))
            grad_score = (chance * (grad_chance - stat[1:2, :])).astype(jnp.bfloat16)
            value_sum = value_sum + matmul(chance.astype(jnp.bfloat16), qg[block, 1], NN_DIMS)
            key_sum = key_sum + matmul(grad_score, qg[block, 0], NN_DIMS)
        key_acc[...] = key_sum
        value_acc[...] = value_sum

    each_group(number, BACKWARD_GROUP, step)
    key_out[...] = (key_acc[...] * SCALE).astype(key_out.dtype)
    value_out[...] = value_acc[...].astype(value_out.dtype)


def call(kernel, name, out_shape, scratch):
    smem = pl.BlockSpec(memory_space=pltpu.SMEM)
    vmem = pl.BlockSpec(memory_space=pltpu.VMEM)
    area = PLACES * ROWS * ROWS

    def run(*operands):
        return pl.pallas_call(
            kernel,
            out_shape=out_shape,
            in_specs=[smem] + [vmem] * (len(operands) - 1),
            out_specs=jax.tree.map(lambda _: vmem, out_shape),
            scratch_shapes=scratch,
            compiler_params=pltpu.CompilerParams(vmem_limit_bytes=VMEM_LIMIT),
            cost_estimate=pl.CostEstimate(
                flops=area * DEPTH * 8, transcendentals=area, bytes_accessed=PLACES * ROWS * DEPTH * 4
            ),
            name=name,
        )(*operands)

    return run


def join(parts, *after):
    count = len(parts)
    starts = np.cumsum([0] + [x.shape[0] for x in parts])

    def kernel(*refs):
        out = refs[-1]
        for i in range(count):
            out[int(starts[i]) : int(starts[i + 1])] = refs[i][...]

    vmem = pl.BlockSpec(memory_space=pltpu.VMEM)
    anywhere = pl.BlockSpec(memory_space=pl.ANY)
    return pl.pallas_call(
        kernel,
        out_shape=jax.ShapeDtypeStruct((int(starts[-1]),) + parts[0].shape[1:], parts[0].dtype),
        in_specs=[vmem] * count + [anywhere] * len(after),
        out_specs=vmem,
        compiler_params=pltpu.CompilerParams(vmem_limit_bytes=VMEM_LIMIT),
        name="join",
    )(*parts, *after)


def last_two(own, *after):
    def kernel(*refs):
        refs[-1][...] = refs[0][:, 2:]

    vmem = pl.BlockSpec(memory_space=pltpu.VMEM)
    anywhere = pl.BlockSpec(memory_space=pl.ANY)
    return pl.pallas_call(
        kernel,
        out_shape=jax.ShapeDtypeStruct((1, 2, ROWS, DEPTH), own.dtype),
        in_specs=[vmem] + [anywhere] * len(after),
        out_specs=vmem,
        compiler_params=pltpu.CompilerParams(vmem_limit_bytes=VMEM_LIMIT),
        name="last_two",
    )(own, *after)


def kernels():
    wide = jax.ShapeDtypeStruct((ROWS, DEPTH), jnp.float32)
    narrow = jax.ShapeDtypeStruct((ROWS, DEPTH), jnp.bfloat16)
    stat_shape = jax.ShapeDtypeStruct((STAT_ROWS, DEPTH), jnp.bfloat16)
    stat_scratch = pltpu.VMEM((STAT_ROWS, DEPTH), jnp.float32)
    blocks = pltpu.VMEM((PLACES, 2, ROWS, DEPTH), jnp.bfloat16)
    stats = pltpu.VMEM((PLACES, 8, ROWS), jnp.float32)
    wide_scratch = pltpu.VMEM((ROWS, DEPTH), jnp.float32)
    return (
        call(
            forward,
            "forward",
            (narrow, stat_shape, wide, wide),
            [blocks] + [wide_scratch] * 3 + [stat_scratch],
        ),
        call(query_side, "query_side", narrow, [blocks, wide_scratch]),
        call(key_side, "key_side", (narrow, narrow), [blocks, stats] + [wide_scratch] * 2),
    )


def on_device(queries, keys, values, out_grad, window_extent, pair_table):
    out_block = queries.shape
    q, k, v, g = (x.reshape(ROWS, DEPTH) for x in (queries, keys, values, out_grad))
    flags = allowed_slots(window_extent, pair_table)
    run_forward, run_query, run_key = kernels()

    kv = jnp.stack([k, v])[None]
    kv_planes = swap(kv, "ta")
    own = join([kv[0], q[None], g[None]])[None]
    near_row = join([own] + swap(own, "wa"))
    near = [near_row] + swap(near_row, "ha")
    kv_middle = join(kv_planes)
    kv_row = join([kv_middle] + swap(kv_middle, "wa"))
    kv_rest = [kv_row] + swap(kv_row, "ha")
    qg_planes = swap(last_two(own, kv_row), "ta")
    attended, stat, norm, delta = run_forward(flags, q, g, *near, *kv_rest)
    pieces = []
    for plane, plane_stat in zip(qg_planes, swap(stat, "ta")):
        pieces += [plane.reshape(2 * ROWS, DEPTH), plane_stat]
    line = join(pieces + [stat])[None]
    qg_row = join([line] + swap(line, "wa"))
    qg_rest = [qg_row] + swap(qg_row, "ha")
    query_grad = run_query(flags, q, g, norm, delta, *near, *kv_rest)
    key_grad, value_grad = run_key(flags, k, v, *near, *qg_rest)
    return tuple(x.reshape(out_block) for x in (attended, query_grad, key_grad, value_grad))


def solution(mesh):
    split = P("ta", "ha", "wa", None)
    return jax.shard_map(
        on_device,
        mesh=mesh,
        in_specs=(split, split, split, split, P(), P()),
        out_specs=(split, split, split, split),
        check_vma=False,
    )
```

```python
import math

import jax
import jax.numpy as jnp
import numpy as np
from jax import lax
from jax.experimental import pallas as pl
from jax.experimental.pallas import tpu as pltpu
from jax.sharding import PartitionSpec as P

ROWS = 384
DEPTH = 128
SCALE = DEPTH ** -0.5
LOG2E = 1.4426950408889634
SCALE2 = SCALE * LOG2E
PLACES = 27
STAT_ROWS = 32
BLOCK_ROWS = 2 * ROWS + STAT_ROWS
LINE_ROWS = 2 * BLOCK_ROWS + STAT_ROWS
NEAR_GROUP = 4
REST_GROUP = 5
BACKWARD_GROUP = 3
MASKED = 1e30
VMEM_LIMIT = 24 * 1024 * 1024
JOIN_LIMIT = 8 * 1024 * 1024

OFFSETS = np.array(
    [[a - 1, b - 1, c - 1] for a in range(3) for b in range(3) for c in range(3)], dtype=np.int32
)
NT_DIMS = (((1,), (1,)), ((), ()))
NN_DIMS = (((1,), (0,)), ((), ()))


def swap(value, axis):
    size = lax.axis_size(axis)
    results = []
    for first in (0, 1):
        pairs = []
        for i in range(first, size - 1, 2):
            pairs += [(i, i + 1), (i + 1, i)]
        results.append(lax.ppermute(value, axis, pairs))
    return results


def allowed_slots(window_extent, pair_table):
    counts = window_extent.shape[:3]
    coords = (lax.axis_index("ta"), lax.axis_index("ha"), lax.axis_index("wa"))
    distance = jnp.abs(jnp.asarray(OFFSETS))
    inside = jnp.ones((27,), jnp.bool_)
    for axis in range(3):
        position = coords[axis] + jnp.asarray(OFFSETS[:, axis])
        inside = inside & (position >= 0) & (position < counts[axis])
    padded = jnp.pad(window_extent, ((1, 1), (1, 1), (1, 1), (0, 0)))
    near = lax.dynamic_slice(padded, coords + (jnp.int32(0),), (3, 3, 3, 3)).reshape(27, 3)
    kept = pair_table[0] == 1
    as_query = kept & inside & jnp.all(distance <= near[13][None, :], axis=1)
    as_key = kept[::-1] & inside & jnp.all(distance <= near, axis=1)
    both = jnp.stack([as_query, as_key]).astype(jnp.int32)
    place = jnp.zeros((3, 3, 3), jnp.int32)
    for axis, weight in ((0, 9), (1, 3), (2, 1)):
        sign = 1 - 2 * (coords[axis] % 2)
        shape = [1, 1, 1]
        shape[axis] = 3
        step = jnp.asarray(np.array([0, 1, -1], dtype=np.int32)) * sign + 1
        place = place + weight * step.reshape(shape)
    place = place.reshape(27)
    hot = place[:, None] == jnp.arange(27, dtype=jnp.int32)[None, :]
    slots = jnp.sum(jnp.where(hot[None], both[:, None, :], 0), axis=2)
    query_slots = slots[0].reshape(3, 9)
    return jnp.concatenate(
        [
            query_slots[0],
            query_slots[1:].T.reshape(18),
            slots[1].reshape(3, 9).T.reshape(PLACES),
        ]
    )


def matmul(left, right, dims):
    return lax.dot_general(left, right, dims, preferred_element_type=jnp.float32)


def thirds(wide):
    return [wide[:, i * DEPTH : (i + 1) * DEPTH] for i in range(ROWS // DEPTH)]


def each_flag(flags, first, count, place, act):
    def body(i, place):
        flag = flags[first + i]

        @pl.when(flag == 1)
        def _():
            act(i, place)

        return place + flag

    return lax.fori_loop(0, count, body, place)


def collect(flags, held, remote, kv, sems):
    data = pl.ds(0, 2 * ROWS)
    ready = jnp.int32(0)
    for _, first, count in held:
        for i in range(count):
            ready = ready + flags[first + i]
    number = ready
    for part, first, count in remote:

        def start(i, place, part=part):
            pltpu.make_async_copy(part.at[i, data], kv.at[place], sems.at[place]).start()

        number = each_flag(flags, first, count, number, start)
    place = jnp.int32(0)
    for part, first, count in held:

        def move(i, place, part=part):
            kv[place] = part[i, : 2 * ROWS]

        place = each_flag(flags, first, count, place, move)

    def wait(at):
        @pl.when(at >= ready)
        def _():
            pltpu.make_async_copy(kv.at[at], kv.at[at], sems.at[at]).wait()

    return number, wait


def no_wait(at):
    del at


def each_group(number, size, wait, step):
    def body(group, carry):
        blocks, biases = [], []
        for k in range(size):
            at = group * size + k

            @pl.when(at < number)
            def _(at=at):
                wait(at)

            blocks.append(jnp.minimum(at, number - 1))
            biases.append(jnp.where(at < number, 0.0, MASKED).astype(jnp.float32))
        step(blocks, biases)
        return carry

    lax.fori_loop(0, lax.div(number + size - 1, size), body, 0)


def forward_groups(number, size, wait, q_ref, kv, peak, total, acc):
    def step(blocks, biases):
        query = q_ref[...]
        scores = [matmul(query, kv[b, :ROWS], NT_DIMS) for b in blocks]
        old = peak[...]
        best = old
        for score, bias in zip(scores, biases):
            a, b, c = thirds(score)
            best = jnp.maximum(best, jnp.maximum(jnp.maximum(a, b), c) - bias)
        new = jnp.broadcast_to(jnp.max(best, axis=1, keepdims=True), best.shape)
        peak[...] = new
        shrink = jnp.exp2((old - new) * SCALE2)
        norm = new * SCALE2
        whole = total[...] * shrink
        mixed = acc[...] * shrink
        for block, score, bias in zip(blocks, scores, biases):
            at = norm + bias
            a, b, c = (jnp.exp2(x * SCALE2 - at) for x in thirds(score))
            whole = whole + (a + b + c)
            chance = jnp.concatenate([x.astype(jnp.bfloat16) for x in (a, b, c)], axis=1)
            mixed = mixed + matmul(chance, kv[block, ROWS:], NN_DIMS)
        total[...] = whole
        acc[...] = mixed

    each_group(number, size, wait, step)


def forward_near(flags, q_ref, n0, n1, n2, peak, total, acc, kv, sems):
    number, wait = collect(flags, [(n0, 0, 3)], [(n1, 3, 3), (n2, 6, 3)], kv, sems)
    peak[...] = jnp.full(peak.shape, -MASKED, jnp.float32)
    total[...] = jnp.zeros(total.shape, jnp.float32)
    acc[...] = jnp.zeros(acc.shape, jnp.float32)
    forward_groups(number, NEAR_GROUP, wait, q_ref, kv, peak, total, acc)


def forward_rest(
    flags, q_ref, g_ref, s0, s1, s2, peak_in, total_in, acc_in,
    out_ref, stat_ref, norm_ref, delta_ref, kv, sems, peak, total, acc, stat,
):
    number, wait = collect(flags, [(s0, 9, 6)], [(s1, 15, 6), (s2, 21, 6)], kv, sems)
    peak[...] = peak_in[...]
    total[...] = total_in[...]
    acc[...] = acc_in[...]
    forward_groups(number, REST_GROUP, wait, q_ref, kv, peak, total, acc)
    whole = jnp.sum(total[...], axis=1, keepdims=True)
    mixed = acc[...] / whole
    out_ref[...] = mixed.astype(out_ref.dtype)
    delta = jnp.sum(mixed * g_ref[...].astype(jnp.float32), axis=1, keepdims=True)
    norm = peak[:, :1] * SCALE2 + jnp.log2(whole)
    lane = lax.broadcasted_iota(jnp.int32, (ROWS, DEPTH), 1)
    both = jnp.where(lane == 0, norm, delta).T[:8]
    stat[...] = jnp.zeros(stat.shape, jnp.float32)
    for kind in range(2):
        left = both[kind : kind + 1]
        for part in range(3):
            rounded = left.astype(jnp.bfloat16).astype(jnp.float32)
            left = left - rounded
            for c, piece in enumerate(thirds(rounded)):
                row = 9 * kind + 3 * part + c
                stat[row : row + 1] = piece
    stat_ref[...] = stat[...].astype(stat_ref.dtype)
    norm_ref[...] = jnp.broadcast_to(norm - math.log2(SCALE), norm_ref.shape)
    delta_ref[...] = jnp.broadcast_to(delta, delta_ref.shape)


def query_side(
    flags, q_ref, g_ref, norm_ref, delta_ref, n0, s0, n1, n2, s1, s2, out_ref, kv, sems, acc
):
    held = [(n0, 0, 3), (s0, 9, 6)]
    remote = [(n1, 3, 3), (n2, 6, 3), (s1, 15, 6), (s2, 21, 6)]
    number, wait = collect(flags, held, remote, kv, sems)
    acc[...] = jnp.zeros(acc.shape, jnp.float32)

    def step(blocks, biases):
        query, grad = q_ref[...], g_ref[...]
        norm, delta = norm_ref[...], delta_ref[...]
        scores = [matmul(query, kv[b, :ROWS], NT_DIMS) for b in blocks]
        grad_chances = [matmul(grad, kv[b, ROWS:], NT_DIMS) for b in blocks]
        sum_of = acc[...]
        for block, score, grad_chance, bias in zip(blocks, scores, grad_chances, biases):
            at = norm + bias
            parts = [
                (jnp.exp2(x * SCALE2 - at) * (y - delta)).astype(jnp.bfloat16)
                for x, y in zip(thirds(score), thirds(grad_chance))
            ]
            sum_of = sum_of + matmul(jnp.concatenate(parts, axis=1), kv[block, :ROWS], NN_DIMS)
        acc[...] = sum_of

    each_group(number, BACKWARD_GROUP, wait, step)
    out_ref[...] = acc[...].astype(out_ref.dtype)


def stat_rows(stat):
    for kind in range(2):
        pieces = []
        for row in range(9 * kind, 9 * kind + 3):
            pieces.append(stat[row : row + 1] + (stat[row + 3 : row + 4] + stat[row + 6 : row + 7]))
        yield jnp.concatenate(pieces, axis=1)


def key_side(
    flags, k_ref, v_ref, n0, l0, l1, l2, m0, m1, m2, n1, n2, key_out, value_out, qg, sems, key_acc, value_acc
):
    slots = []
    for near, line, columns in ((n0, l0, m0), (n1, l1, m1), (n2, l2, m2)):
        for w, rows in enumerate((line, columns.at[0], columns.at[1])):
            slots += [(near, w, rows, t) for t in range(3)]
    data = pl.ds(0, 2 * ROWS)

    def each_slot(act):
        place = jnp.int32(0)
        for at, (near, w, rows, t) in enumerate(slots):
            flag = flags[PLACES + at]
            pl.when(flag == 1)(lambda place=place, slot=(near, w, rows, t): act(place, *slot))
            place = place + flag
        return place

    def start(place, near, w, rows, t):
        if t == 0 and near is not n0:
            source = near.at[w, pl.ds(2 * ROWS, 2 * ROWS)]
            pltpu.make_async_copy(source, qg.at[place, data], sems.at[place]).start()

    def move(place, near, w, rows, t):
        if t > 0:
            qg[place] = rows[BLOCK_ROWS * (t - 1) : BLOCK_ROWS * t]
        else:
            qg[place, 2 * ROWS :] = rows[2 * BLOCK_ROWS :]
            if near is n0:
                qg[place, : 2 * ROWS] = near[w, 2 * ROWS :]

    def wait(place, near, w, rows, t):
        if t == 0 and near is not n0:
            pltpu.make_async_copy(qg.at[place, data], qg.at[place, data], sems.at[place]).wait()

    each_slot(start)
    number = each_slot(move)
    each_slot(wait)
    key_acc[...] = jnp.zeros(key_acc.shape, jnp.float32)
    value_acc[...] = jnp.zeros(value_acc.shape, jnp.float32)

    def step(blocks, biases):
        key, value = k_ref[...], v_ref[...]
        scores = [matmul(key, qg[b, :ROWS], NT_DIMS) for b in blocks]
        grad_chances = [matmul(value, qg[b, ROWS : 2 * ROWS], NT_DIMS) for b in blocks]
        key_sum, value_sum = key_acc[...], value_acc[...]
        for block, score, grad_chance, bias in zip(blocks, scores, grad_chances, biases):
            norm, delta = stat_rows(qg[block, 2 * ROWS :].astype(jnp.float32))
            chance = jnp.exp2(score * SCALE2 - (norm + bias))
            grad_score = (chance * (grad_chance - delta)).astype(jnp.bfloat16)
            value_sum = value_sum + matmul(chance.astype(jnp.bfloat16), qg[block, ROWS : 2 * ROWS], NN_DIMS)
            key_sum = key_sum + matmul(grad_score, qg[block, :ROWS], NN_DIMS)
        key_acc[...] = key_sum
        value_acc[...] = value_sum

    each_group(number, BACKWARD_GROUP, no_wait, step)
    key_out[...] = (key_acc[...] * SCALE).astype(key_out.dtype)
    value_out[...] = value_acc[...].astype(value_out.dtype)


def call(kernel, name, halo, out_shape, scratch):
    smem = pl.BlockSpec(memory_space=pltpu.SMEM)
    vmem = pl.BlockSpec(memory_space=pltpu.VMEM)
    anywhere = pl.BlockSpec(memory_space=pl.ANY)
    area = PLACES * ROWS * ROWS

    def run(*operands):
        return pl.pallas_call(
            kernel,
            out_shape=out_shape,
            in_specs=[smem]
            + [anywhere if i in halo else vmem for i in range(1, len(operands))],
            out_specs=jax.tree.map(lambda _: vmem, out_shape),
            scratch_shapes=scratch,
            compiler_params=pltpu.CompilerParams(vmem_limit_bytes=VMEM_LIMIT),
            cost_estimate=pl.CostEstimate(
                flops=area * DEPTH * 8, transcendentals=area, bytes_accessed=PLACES * ROWS * DEPTH * 4
            ),
            name=name,
        )(*operands)

    return run


def join(parts, *after):
    count = len(parts)
    starts = np.cumsum([0] + [x.shape[0] for x in parts])

    def kernel(*refs):
        out = refs[-1]
        for i in range(count):
            out[int(starts[i]) : int(starts[i + 1])] = refs[i][...]

    vmem = pl.BlockSpec(memory_space=pltpu.VMEM)
    anywhere = pl.BlockSpec(memory_space=pl.ANY)
    return pl.pallas_call(
        kernel,
        out_shape=jax.ShapeDtypeStruct((int(starts[-1]),) + parts[0].shape[1:], parts[0].dtype),
        in_specs=[vmem] * count + [anywhere] * len(after),
        out_specs=vmem,
        compiler_params=pltpu.CompilerParams(vmem_limit_bytes=JOIN_LIMIT),
        name="join",
    )(*parts, *after)


def last_two(own, *after):
    def kernel(*refs):
        refs[-1][...] = refs[0][:, 2:]

    vmem = pl.BlockSpec(memory_space=pltpu.VMEM)
    anywhere = pl.BlockSpec(memory_space=pl.ANY)
    return pl.pallas_call(
        kernel,
        out_shape=jax.ShapeDtypeStruct((1, 2, ROWS, DEPTH), own.dtype),
        in_specs=[vmem] + [anywhere] * len(after),
        out_specs=vmem,
        compiler_params=pltpu.CompilerParams(vmem_limit_bytes=JOIN_LIMIT),
        name="last_two",
    )(own, *after)


def kernels():
    wide = jax.ShapeDtypeStruct((ROWS, DEPTH), jnp.float32)
    narrow = jax.ShapeDtypeStruct((ROWS, DEPTH), jnp.bfloat16)
    stat_shape = jax.ShapeDtypeStruct((STAT_ROWS, DEPTH), jnp.bfloat16)
    stat_scratch = pltpu.VMEM((STAT_ROWS, DEPTH), jnp.float32)
    blocks = pltpu.VMEM((PLACES, 2 * ROWS, DEPTH), jnp.bfloat16)
    stat_blocks = pltpu.VMEM((PLACES, BLOCK_ROWS, DEPTH), jnp.bfloat16)
    sems = pltpu.SemaphoreType.DMA((PLACES,))
    wide_scratch = pltpu.VMEM((ROWS, DEPTH), jnp.float32)
    return (
        call(forward_near, "forward_near", range(3, 5), (wide, wide, wide), [blocks, sems]),
        call(
            forward_rest,
            "forward_rest",
            range(4, 6),
            (narrow, stat_shape, wide, wide),
            [blocks, sems] + [wide_scratch] * 3 + [stat_scratch],
        ),
        call(query_side, "query_side", range(7, 11), narrow, [blocks, sems, wide_scratch]),
        call(
            key_side,
            "key_side",
            range(10, 12),
            (narrow, narrow),
            [stat_blocks, sems] + [wide_scratch] * 2,
        ),
    )


def on_device(queries, keys, values, out_grad, window_extent, pair_table):
    out_block = queries.shape
    q, k, v, g = (x.reshape(ROWS, DEPTH) for x in (queries, keys, values, out_grad))
    flags = allowed_slots(window_extent, pair_table)
    run_near, run_rest, run_query, run_key = kernels()

    kv = jnp.stack([k, v])[None]
    kv_planes = swap(kv, "ta")
    own = join([kv[0], q[None], g[None]])[None]
    near_row = join([own] + swap(own, "wa"))
    near = [x.reshape(3, 4 * ROWS, DEPTH) for x in [near_row] + swap(near_row, "ha")]
    kv_middle = join(kv_planes)
    kv_row = join([kv_middle] + swap(kv_middle, "wa"))
    kv_rest = [x.reshape(6, 2 * ROWS, DEPTH) for x in [kv_row] + swap(kv_row, "ha")]
    qg_planes = swap(last_two(own, kv_row), "ta")
    state = run_near(flags, q, *near)
    attended, stat, norm, delta = run_rest(flags, q, g, *kv_rest, *state)
    pieces = []
    for plane, plane_stat in zip(qg_planes, swap(stat, "ta")):
        pieces += [plane.reshape(2 * ROWS, DEPTH), plane_stat]
    line = join(pieces + [stat])
    sides = swap(line, "wa")
    lines = [line] + swap(line, "ha")
    columns = join([x[None] for x in sides], *lines[1:])
    columns = [columns] + swap(columns, "ha")
    query_grad = run_query(
        flags, q, g, norm, delta, near[0], kv_rest[0], *near[1:], *kv_rest[1:]
    )
    key_grad, value_grad = run_key(flags, k, v, near[0], *lines, *columns, *near[1:])
    return tuple(x.reshape(out_block) for x in (attended, query_grad, key_grad, value_grad))


def solution(mesh):
    split = P("ta", "ha", "wa", None)
    return jax.shard_map(
        on_device,
        mesh=mesh,
        in_specs=(split, split, split, split, P(), P()),
        out_specs=(split, split, split, split),
        check_vma=False,
    )
```

```python
import math

import jax
import jax.numpy as jnp
import numpy as np
from jax import lax
from jax.experimental import pallas as pl
from jax.experimental.pallas import tpu as pltpu
from jax.sharding import PartitionSpec as P

ROWS = 384
DEPTH = 128
SCALE = DEPTH ** -0.5
LOG2E = 1.4426950408889634
SCALE2 = SCALE * LOG2E
PLACES = 27
STAT_ROWS = 32
BLOCK_ROWS = 2 * ROWS + STAT_ROWS
LINE_ROWS = 2 * BLOCK_ROWS + STAT_ROWS
NEAR_GROUP = 4
REST_GROUP = 5
BACKWARD_GROUP = 6
BACKWARD_TAIL = 3
MASKED = 1e30
VMEM_LIMIT = 24 * 1024 * 1024
JOIN_LIMIT = 8 * 1024 * 1024

OFFSETS = np.array(
    [[a - 1, b - 1, c - 1] for a in range(3) for b in range(3) for c in range(3)], dtype=np.int32
)
NT_DIMS = (((1,), (1,)), ((), ()))
NN_DIMS = (((1,), (0,)), ((), ()))


def swap(value, axis):
    size = lax.axis_size(axis)
    results = []
    for first in (0, 1):
        pairs = []
        for i in range(first, size - 1, 2):
            pairs += [(i, i + 1), (i + 1, i)]
        results.append(lax.ppermute(value, axis, pairs))
    return results


def allowed_slots(window_extent, pair_table):
    counts = window_extent.shape[:3]
    coords = (lax.axis_index("ta"), lax.axis_index("ha"), lax.axis_index("wa"))
    distance = jnp.abs(jnp.asarray(OFFSETS))
    inside = jnp.ones((27,), jnp.bool_)
    for axis in range(3):
        position = coords[axis] + jnp.asarray(OFFSETS[:, axis])
        inside = inside & (position >= 0) & (position < counts[axis])
    padded = jnp.pad(window_extent, ((1, 1), (1, 1), (1, 1), (0, 0)))
    near = lax.dynamic_slice(padded, coords + (jnp.int32(0),), (3, 3, 3, 3)).reshape(27, 3)
    kept = pair_table[0] == 1
    as_query = kept & inside & jnp.all(distance <= near[13][None, :], axis=1)
    as_key = kept[::-1] & inside & jnp.all(distance <= near, axis=1)
    both = jnp.stack([as_query, as_key]).astype(jnp.int32)
    place = jnp.zeros((3, 3, 3), jnp.int32)
    for axis, weight in ((0, 9), (1, 3), (2, 1)):
        sign = 1 - 2 * (coords[axis] % 2)
        shape = [1, 1, 1]
        shape[axis] = 3
        step = jnp.asarray(np.array([0, 1, -1], dtype=np.int32)) * sign + 1
        place = place + weight * step.reshape(shape)
    place = place.reshape(27)
    hot = place[:, None] == jnp.arange(27, dtype=jnp.int32)[None, :]
    slots = jnp.sum(jnp.where(hot[None], both[:, None, :], 0), axis=2)
    query_slots = slots[0].reshape(3, 9)
    return jnp.concatenate(
        [
            query_slots[0],
            query_slots[1:].T.reshape(18),
            slots[1].reshape(3, 9).T.reshape(PLACES),
        ]
    )


def matmul(left, right, dims):
    return lax.dot_general(left, right, dims, preferred_element_type=jnp.float32)


def thirds(wide):
    return [wide[:, i * DEPTH : (i + 1) * DEPTH] for i in range(ROWS // DEPTH)]


def each_flag(flags, first, count, place, act):
    def body(i, place):
        flag = flags[first + i]

        @pl.when(flag == 1)
        def _():
            act(i, place)

        return place + flag

    return lax.fori_loop(0, count, body, place)


def collect(flags, held, remote, kv, sems):
    data = pl.ds(0, 2 * ROWS)
    ready = jnp.int32(0)
    for _, first, count in held:
        for i in range(count):
            ready = ready + flags[first + i]
    number = ready
    for part, first, count in remote:

        def start(i, place, part=part):
            pltpu.make_async_copy(part.at[i, data], kv.at[place], sems.at[place]).start()

        number = each_flag(flags, first, count, number, start)
    place = jnp.int32(0)
    for part, first, count in held:

        def move(i, place, part=part):
            kv[place] = part[i, : 2 * ROWS]

        place = each_flag(flags, first, count, place, move)

    def wait(at):
        @pl.when(at >= ready)
        def _():
            pltpu.make_async_copy(kv.at[at], kv.at[at], sems.at[at]).wait()

    return number, wait


def no_wait(at):
    del at


def each_group(number, size, wait, step, tail=None):
    def run(first, count):
        blocks, biases = [], []
        for k in range(count):
            at = first + k

            @pl.when(at < number)
            def _(at=at):
                wait(at)

            blocks.append(jnp.minimum(at, number - 1))
            biases.append(jnp.where(at < number, 0.0, MASKED).astype(jnp.float32))
        step(blocks, biases)

    def body(group, carry):
        run(group * size, size)
        return carry

    if tail is None:
        lax.fori_loop(0, lax.div(number + size - 1, size), body, 0)
        return
    whole = lax.div(number + size - tail - 1, size)
    lax.fori_loop(0, whole, body, 0)

    @pl.when(whole * size < number)
    def _():
        run(whole * size, tail)


def forward_groups(number, size, wait, q_ref, kv, peak, total, acc):
    def step(blocks, biases):
        query = q_ref[...]
        scores = [matmul(query, kv[b, :ROWS], NT_DIMS) for b in blocks]
        old = peak[...]
        best = old
        for score, bias in zip(scores, biases):
            a, b, c = thirds(score)
            best = jnp.maximum(best, jnp.maximum(jnp.maximum(a, b), c) - bias)
        new = jnp.broadcast_to(jnp.max(best, axis=1, keepdims=True), best.shape)
        peak[...] = new
        shrink = jnp.exp2((old - new) * SCALE2)
        norm = new * SCALE2
        whole = total[...] * shrink
        mixed = acc[...] * shrink
        for block, score, bias in zip(blocks, scores, biases):
            at = norm + bias
            a, b, c = (jnp.exp2(x * SCALE2 - at) for x in thirds(score))
            whole = whole + (a + b + c)
            chance = jnp.concatenate([x.astype(jnp.bfloat16) for x in (a, b, c)], axis=1)
            mixed = mixed + matmul(chance, kv[block, ROWS:], NN_DIMS)
        total[...] = whole
        acc[...] = mixed

    each_group(number, size, wait, step)


def forward_near(flags, q_ref, n0, n1, n2, peak, total, acc, kv, sems):
    number, wait = collect(flags, [(n0, 0, 3)], [(n1, 3, 3), (n2, 6, 3)], kv, sems)
    peak[...] = jnp.full(peak.shape, -MASKED, jnp.float32)
    total[...] = jnp.zeros(total.shape, jnp.float32)
    acc[...] = jnp.zeros(acc.shape, jnp.float32)
    forward_groups(number, NEAR_GROUP, wait, q_ref, kv, peak, total, acc)


def forward_rest(
    flags, q_ref, g_ref, s0, s1, s2, peak_in, total_in, acc_in,
    out_ref, stat_ref, norm_ref, delta_ref, kv, sems, peak, total, acc, stat,
):
    number, wait = collect(flags, [(s0, 9, 6)], [(s1, 15, 6), (s2, 21, 6)], kv, sems)
    peak[...] = peak_in[...]
    total[...] = total_in[...]
    acc[...] = acc_in[...]
    forward_groups(number, REST_GROUP, wait, q_ref, kv, peak, total, acc)
    whole = jnp.sum(total[...], axis=1, keepdims=True)
    mixed = acc[...] / whole
    out_ref[...] = mixed.astype(out_ref.dtype)
    delta = jnp.sum(mixed * g_ref[...].astype(jnp.float32), axis=1, keepdims=True)
    norm = peak[:, :1] * SCALE2 + jnp.log2(whole)
    lane = lax.broadcasted_iota(jnp.int32, (ROWS, DEPTH), 1)
    both = jnp.where(lane == 0, norm, delta).T[:8]
    stat[...] = jnp.zeros(stat.shape, jnp.float32)
    for kind in range(2):
        left = both[kind : kind + 1]
        for part in range(3):
            rounded = left.astype(jnp.bfloat16).astype(jnp.float32)
            left = left - rounded
            for c, piece in enumerate(thirds(rounded)):
                row = 9 * kind + 3 * part + c
                stat[row : row + 1] = piece
    stat_ref[...] = stat[...].astype(stat_ref.dtype)
    norm_ref[...] = jnp.broadcast_to(norm - math.log2(SCALE), norm_ref.shape)
    delta_ref[...] = jnp.broadcast_to(delta, delta_ref.shape)


def query_side(
    flags, q_ref, g_ref, norm_ref, delta_ref, n0, s0, n1, n2, s1, s2, out_ref, kv, sems, acc
):
    held = [(n0, 0, 3), (s0, 9, 6)]
    remote = [(n1, 3, 3), (n2, 6, 3), (s1, 15, 6), (s2, 21, 6)]
    number, wait = collect(flags, held, remote, kv, sems)
    acc[...] = jnp.zeros(acc.shape, jnp.float32)

    def step(blocks, biases):
        query, grad = q_ref[...], g_ref[...]
        norm, delta = norm_ref[...], delta_ref[...]
        scores = [matmul(query, kv[b, :ROWS], NT_DIMS) for b in blocks]
        grad_chances = [matmul(grad, kv[b, ROWS:], NT_DIMS) for b in blocks]
        sum_of = acc[...]
        for block, score, grad_chance, bias in zip(blocks, scores, grad_chances, biases):
            at = norm + bias
            parts = [
                (jnp.exp2(x * SCALE2 - at) * (y - delta)).astype(jnp.bfloat16)
                for x, y in zip(thirds(score), thirds(grad_chance))
            ]
            sum_of = sum_of + matmul(jnp.concatenate(parts, axis=1), kv[block, :ROWS], NN_DIMS)
        acc[...] = sum_of

    each_group(number, BACKWARD_GROUP, wait, step, BACKWARD_TAIL)
    out_ref[...] = acc[...].astype(out_ref.dtype)


def stat_rows(stat):
    for kind in range(2):
        pieces = []
        for row in range(9 * kind, 9 * kind + 3):
            pieces.append(stat[row : row + 1] + (stat[row + 3 : row + 4] + stat[row + 6 : row + 7]))
        yield jnp.concatenate(pieces, axis=1)


def key_side(
    flags, k_ref, v_ref, n0, l0, l1, l2, m0, m1, m2, n1, n2, key_out, value_out, qg, sems, key_acc, value_acc
):
    slots = []
    for near, line, columns in ((n0, l0, m0), (n1, l1, m1), (n2, l2, m2)):
        for w, rows in enumerate((line, columns.at[0], columns.at[1])):
            slots += [(near, w, rows, t) for t in range(3)]
    data = pl.ds(0, 2 * ROWS)

    def each_slot(act):
        place = jnp.int32(0)
        for at, (near, w, rows, t) in enumerate(slots):
            flag = flags[PLACES + at]
            pl.when(flag == 1)(lambda place=place, slot=(near, w, rows, t): act(place, *slot))
            place = place + flag
        return place

    def start(place, near, w, rows, t):
        if t == 0 and near is not n0:
            source = near.at[w, pl.ds(2 * ROWS, 2 * ROWS)]
            pltpu.make_async_copy(source, qg.at[place, data], sems.at[place]).start()

    def move(place, near, w, rows, t):
        if t > 0:
            qg[place] = rows[BLOCK_ROWS * (t - 1) : BLOCK_ROWS * t]
        else:
            qg[place, 2 * ROWS :] = rows[2 * BLOCK_ROWS :]
            if near is n0:
                qg[place, : 2 * ROWS] = near[w, 2 * ROWS :]

    def wait(place, near, w, rows, t):
        if t == 0 and near is not n0:
            pltpu.make_async_copy(qg.at[place, data], qg.at[place, data], sems.at[place]).wait()

    each_slot(start)
    number = each_slot(move)
    each_slot(wait)
    key_acc[...] = jnp.zeros(key_acc.shape, jnp.float32)
    value_acc[...] = jnp.zeros(value_acc.shape, jnp.float32)

    def step(blocks, biases):
        key, value = k_ref[...], v_ref[...]
        scores = [matmul(key, qg[b, :ROWS], NT_DIMS) for b in blocks]
        grad_chances = [matmul(value, qg[b, ROWS : 2 * ROWS], NT_DIMS) for b in blocks]
        key_sum, value_sum = key_acc[...], value_acc[...]
        for block, score, grad_chance, bias in zip(blocks, scores, grad_chances, biases):
            norm, delta = stat_rows(qg[block, 2 * ROWS :].astype(jnp.float32))
            chance = jnp.exp2(score * SCALE2 - (norm + bias))
            grad_score = (chance * (grad_chance - delta)).astype(jnp.bfloat16)
            value_sum = value_sum + matmul(chance.astype(jnp.bfloat16), qg[block, ROWS : 2 * ROWS], NN_DIMS)
            key_sum = key_sum + matmul(grad_score, qg[block, :ROWS], NN_DIMS)
        key_acc[...] = key_sum
        value_acc[...] = value_sum

    each_group(number, BACKWARD_GROUP, no_wait, step, BACKWARD_TAIL)
    key_out[...] = (key_acc[...] * SCALE).astype(key_out.dtype)
    value_out[...] = value_acc[...].astype(value_out.dtype)


def call(kernel, name, halo, out_shape, scratch):
    smem = pl.BlockSpec(memory_space=pltpu.SMEM)
    vmem = pl.BlockSpec(memory_space=pltpu.VMEM)
    anywhere = pl.BlockSpec(memory_space=pl.ANY)
    area = PLACES * ROWS * ROWS

    def run(*operands):
        return pl.pallas_call(
            kernel,
            out_shape=out_shape,
            in_specs=[smem]
            + [anywhere if i in halo else vmem for i in range(1, len(operands))],
            out_specs=jax.tree.map(lambda _: vmem, out_shape),
            scratch_shapes=scratch,
            compiler_params=pltpu.CompilerParams(vmem_limit_bytes=VMEM_LIMIT),
            cost_estimate=pl.CostEstimate(
                flops=area * DEPTH * 8, transcendentals=area, bytes_accessed=PLACES * ROWS * DEPTH * 4
            ),
            name=name,
        )(*operands)

    return run


def join(parts, *after):
    count = len(parts)
    starts = np.cumsum([0] + [x.shape[0] for x in parts])

    def kernel(*refs):
        out = refs[-1]
        for i in range(count):
            out[int(starts[i]) : int(starts[i + 1])] = refs[i][...]

    vmem = pl.BlockSpec(memory_space=pltpu.VMEM)
    anywhere = pl.BlockSpec(memory_space=pl.ANY)
    return pl.pallas_call(
        kernel,
        out_shape=jax.ShapeDtypeStruct((int(starts[-1]),) + parts[0].shape[1:], parts[0].dtype),
        in_specs=[vmem] * count + [anywhere] * len(after),
        out_specs=vmem,
        compiler_params=pltpu.CompilerParams(vmem_limit_bytes=JOIN_LIMIT),
        name="join",
    )(*parts, *after)


def last_two(own, *after):
    def kernel(*refs):
        refs[-1][...] = refs[0][:, 2:]

    vmem = pl.BlockSpec(memory_space=pltpu.VMEM)
    anywhere = pl.BlockSpec(memory_space=pl.ANY)
    return pl.pallas_call(
        kernel,
        out_shape=jax.ShapeDtypeStruct((1, 2, ROWS, DEPTH), own.dtype),
        in_specs=[vmem] + [anywhere] * len(after),
        out_specs=vmem,
        compiler_params=pltpu.CompilerParams(vmem_limit_bytes=JOIN_LIMIT),
        name="last_two",
    )(own, *after)


def kernels():
    wide = jax.ShapeDtypeStruct((ROWS, DEPTH), jnp.float32)
    narrow = jax.ShapeDtypeStruct((ROWS, DEPTH), jnp.bfloat16)
    stat_shape = jax.ShapeDtypeStruct((STAT_ROWS, DEPTH), jnp.bfloat16)
    stat_scratch = pltpu.VMEM((STAT_ROWS, DEPTH), jnp.float32)
    blocks = pltpu.VMEM((PLACES, 2 * ROWS, DEPTH), jnp.bfloat16)
    stat_blocks = pltpu.VMEM((PLACES, BLOCK_ROWS, DEPTH), jnp.bfloat16)
    sems = pltpu.SemaphoreType.DMA((PLACES,))
    wide_scratch = pltpu.VMEM((ROWS, DEPTH), jnp.float32)
    return (
        call(forward_near, "forward_near", range(3, 5), (wide, wide, wide), [blocks, sems]),
        call(
            forward_rest,
            "forward_rest",
            range(4, 6),
            (narrow, stat_shape, wide, wide),
            [blocks, sems] + [wide_scratch] * 3 + [stat_scratch],
        ),
        call(query_side, "query_side", range(7, 11), narrow, [blocks, sems, wide_scratch]),
        call(
            key_side,
            "key_side",
            range(10, 12),
            (narrow, narrow),
            [stat_blocks, sems] + [wide_scratch] * 2,
        ),
    )


def on_device(queries, keys, values, out_grad, window_extent, pair_table):
    out_block = queries.shape
    q, k, v, g = (x.reshape(ROWS, DEPTH) for x in (queries, keys, values, out_grad))
    flags = allowed_slots(window_extent, pair_table)
    run_near, run_rest, run_query, run_key = kernels()

    kv = jnp.stack([k, v])[None]
    kv_planes = swap(kv, "ta")
    own = join([kv[0], q[None], g[None]])[None]
    near_row = join([own] + swap(own, "wa"))
    near = [x.reshape(3, 4 * ROWS, DEPTH) for x in [near_row] + swap(near_row, "ha")]
    kv_middle = join(kv_planes)
    kv_row = join([kv_middle] + swap(kv_middle, "wa"))
    kv_rest = [x.reshape(6, 2 * ROWS, DEPTH) for x in [kv_row] + swap(kv_row, "ha")]
    qg_planes = swap(last_two(own, kv_row), "ta")
    state = run_near(flags, q, *near)
    attended, stat, norm, delta = run_rest(flags, q, g, *kv_rest, *state)
    pieces = []
    for plane, plane_stat in zip(qg_planes, swap(stat, "ta")):
        pieces += [plane.reshape(2 * ROWS, DEPTH), plane_stat]
    line = join(pieces + [stat])
    sides = swap(line, "wa")
    lines = [line] + swap(line, "ha")
    columns = join([x[None] for x in sides], *lines[1:])
    columns = [columns] + swap(columns, "ha")
    query_grad = run_query(
        flags, q, g, norm, delta, near[0], kv_rest[0], *near[1:], *kv_rest[1:]
    )
    key_grad, value_grad = run_key(flags, k, v, near[0], *lines, *columns, *near[1:])
    return tuple(x.reshape(out_block) for x in (attended, query_grad, key_grad, value_grad))


def solution(mesh):
    split = P("ta", "ha", "wa", None)
    return jax.shard_map(
        on_device,
        mesh=mesh,
        in_specs=(split, split, split, split, P(), P()),
        out_specs=(split, split, split, split),
        check_vma=False,
    )
```

```python
import math

import jax
import jax.numpy as jnp
import numpy as np
from jax import lax
from jax.experimental import pallas as pl
from jax.experimental.pallas import tpu as pltpu
from jax.sharding import PartitionSpec as P

ROWS = 384
DEPTH = 128
SCALE = DEPTH ** -0.5
LOG2E = 1.4426950408889634
SCALE2 = SCALE * LOG2E
PLACES = 27
STAT_ROWS = 32
BLOCK_ROWS = 2 * ROWS + STAT_ROWS
LINE_ROWS = 2 * BLOCK_ROWS + STAT_ROWS
NEAR_GROUP = 4
REST_GROUP = 5
BACKWARD_GROUP = 3
MASKED = 1e30
VMEM_LIMIT = 16 * 1024 * 1024
JOIN_LIMIT = 8 * 1024 * 1024

OFFSETS = np.array(
    [[a - 1, b - 1, c - 1] for a in range(3) for b in range(3) for c in range(3)], dtype=np.int32
)
NT_DIMS = (((1,), (1,)), ((), ()))
NN_DIMS = (((1,), (0,)), ((), ()))


def swap(value, axis):
    size = lax.axis_size(axis)
    results = []
    for first in (0, 1):
        pairs = []
        for i in range(first, size - 1, 2):
            pairs += [(i, i + 1), (i + 1, i)]
        results.append(lax.ppermute(value, axis, pairs))
    return results


def allowed_slots(window_extent, pair_table):
    counts = window_extent.shape[:3]
    coords = (lax.axis_index("ta"), lax.axis_index("ha"), lax.axis_index("wa"))
    distance = jnp.abs(jnp.asarray(OFFSETS))
    inside = jnp.ones((27,), jnp.bool_)
    for axis in range(3):
        position = coords[axis] + jnp.asarray(OFFSETS[:, axis])
        inside = inside & (position >= 0) & (position < counts[axis])
    padded = jnp.pad(window_extent, ((1, 1), (1, 1), (1, 1), (0, 0)))
    near = lax.dynamic_slice(padded, coords + (jnp.int32(0),), (3, 3, 3, 3)).reshape(27, 3)
    kept = pair_table[0] == 1
    as_query = kept & inside & jnp.all(distance <= near[13][None, :], axis=1)
    as_key = kept[::-1] & inside & jnp.all(distance <= near, axis=1)
    both = jnp.stack([as_query, as_key]).astype(jnp.int32)
    place = jnp.zeros((3, 3, 3), jnp.int32)
    for axis, weight in ((0, 9), (1, 3), (2, 1)):
        sign = 1 - 2 * (coords[axis] % 2)
        shape = [1, 1, 1]
        shape[axis] = 3
        step = jnp.asarray(np.array([0, 1, -1], dtype=np.int32)) * sign + 1
        place = place + weight * step.reshape(shape)
    place = place.reshape(27)
    hot = place[:, None] == jnp.arange(27, dtype=jnp.int32)[None, :]
    slots = jnp.sum(jnp.where(hot[None], both[:, None, :], 0), axis=2)
    query_slots = slots[0].reshape(3, 9)
    return jnp.concatenate(
        [
            query_slots[0],
            query_slots[1:].T.reshape(18),
            slots[1].reshape(3, 9).T.reshape(PLACES),
        ]
    )


def matmul(left, right, dims):
    return lax.dot_general(left, right, dims, preferred_element_type=jnp.float32)


def thirds(wide):
    return [wide[:, i * DEPTH : (i + 1) * DEPTH] for i in range(ROWS // DEPTH)]


def each_flag(flags, first, count, place, act):
    def body(i, place):
        flag = flags[first + i]

        @pl.when(flag == 1)
        def _():
            act(i, place)

        return place + flag

    return lax.fori_loop(0, count, body, place)


def collect(flags, held, remote, kv, sems):
    data = pl.ds(0, 2 * ROWS)
    ready = jnp.int32(0)
    for _, first, count in held:
        for i in range(count):
            ready = ready + flags[first + i]
    number = ready
    for part, first, count in remote:

        def start(i, place, part=part):
            pltpu.make_async_copy(part.at[i, data], kv.at[place], sems.at[place]).start()

        number = each_flag(flags, first, count, number, start)
    place = jnp.int32(0)
    for part, first, count in held:

        def move(i, place, part=part):
            kv[place] = part[i, : 2 * ROWS]

        place = each_flag(flags, first, count, place, move)

    def wait(at):
        @pl.when(at >= ready)
        def _():
            pltpu.make_async_copy(kv.at[at], kv.at[at], sems.at[at]).wait()

    return number, wait


def no_wait(at):
    del at


def each_group(number, size, wait, step):
    def body(group, carry):
        blocks, biases = [], []
        for k in range(size):
            at = group * size + k

            @pl.when(at < number)
            def _(at=at):
                wait(at)

            blocks.append(jnp.minimum(at, number - 1))
            biases.append(jnp.where(at < number, 0.0, MASKED).astype(jnp.float32))
        step(blocks, biases)
        return carry

    lax.fori_loop(0, lax.div(number + size - 1, size), body, 0)


def forward_groups(number, size, wait, q_ref, kv, peak, total, acc):
    def step(blocks, biases):
        query = q_ref[...]
        scores = [matmul(query, kv[b, :ROWS], NT_DIMS) for b in blocks]
        old = peak[...]
        best = old
        for score, bias in zip(scores, biases):
            a, b, c = thirds(score)
            best = jnp.maximum(best, jnp.maximum(jnp.maximum(a, b), c) - bias)
        new = jnp.broadcast_to(jnp.max(best, axis=1, keepdims=True), best.shape)
        peak[...] = new
        shrink = jnp.exp2((old - new) * SCALE2)
        norm = new * SCALE2
        whole = total[...] * shrink
        mixed = acc[...] * shrink
        for block, score, bias in zip(blocks, scores, biases):
            at = norm + bias
            a, b, c = (jnp.exp2(x * SCALE2 - at) for x in thirds(score))
            whole = whole + (a + b + c)
            chance = jnp.concatenate([x.astype(jnp.bfloat16) for x in (a, b, c)], axis=1)
            mixed = mixed + matmul(chance, kv[block, ROWS:], NN_DIMS)
        total[...] = whole
        acc[...] = mixed

    each_group(number, size, wait, step)


def forward_near(flags, q_ref, n0, n1, n2, peak, total, acc, kv, sems):
    number, wait = collect(flags, [(n0, 0, 3)], [(n1, 3, 3), (n2, 6, 3)], kv, sems)
    peak[...] = jnp.full(peak.shape, -MASKED, jnp.float32)
    total[...] = jnp.zeros(total.shape, jnp.float32)
    acc[...] = jnp.zeros(acc.shape, jnp.float32)
    forward_groups(number, NEAR_GROUP, wait, q_ref, kv, peak, total, acc)


def forward_rest(
    flags, q_ref, g_ref, s0, s1, s2, peak_in, total_in, acc_in,
    out_ref, stat_ref, norm_ref, delta_ref, kv, sems, peak, total, acc, stat,
):
    number, wait = collect(flags, [(s0, 9, 6)], [(s1, 15, 6), (s2, 21, 6)], kv, sems)
    peak[...] = peak_in[...]
    total[...] = total_in[...]
    acc[...] = acc_in[...]
    forward_groups(number, REST_GROUP, wait, q_ref, kv, peak, total, acc)
    whole = jnp.sum(total[...], axis=1, keepdims=True)
    mixed = acc[...] / whole
    out_ref[...] = mixed.astype(out_ref.dtype)
    delta = jnp.sum(mixed * g_ref[...].astype(jnp.float32), axis=1, keepdims=True)
    norm = peak[:, :1] * SCALE2 + jnp.log2(whole)
    lane = lax.broadcasted_iota(jnp.int32, (ROWS, DEPTH), 1)
    both = jnp.where(lane == 0, norm, delta).T[:8]
    stat[...] = jnp.zeros(stat.shape, jnp.float32)
    for kind in range(2):
        left = both[kind : kind + 1]
        for part in range(3):
            rounded = left.astype(jnp.bfloat16).astype(jnp.float32)
            left = left - rounded
            for c, piece in enumerate(thirds(rounded)):
                row = 9 * kind + 3 * part + c
                stat[row : row + 1] = piece
    stat_ref[...] = stat[...].astype(stat_ref.dtype)
    norm_ref[...] = jnp.broadcast_to(norm - math.log2(SCALE), norm_ref.shape)
    delta_ref[...] = jnp.broadcast_to(delta, delta_ref.shape)


def query_side(
    flags, q_ref, g_ref, norm_ref, delta_ref, n0, s0, n1, n2, s1, s2, out_ref, kv, sems, acc
):
    held = [(n0, 0, 3), (s0, 9, 6)]
    remote = [(n1, 3, 3), (n2, 6, 3), (s1, 15, 6), (s2, 21, 6)]
    number, wait = collect(flags, held, remote, kv, sems)
    acc[...] = jnp.zeros(acc.shape, jnp.float32)

    def step(blocks, biases):
        query, grad = q_ref[...], g_ref[...]
        norm, delta = norm_ref[...], delta_ref[...]
        scores = [matmul(query, kv[b, :ROWS], NT_DIMS) for b in blocks]
        grad_chances = [matmul(grad, kv[b, ROWS:], NT_DIMS) for b in blocks]
        sum_of = acc[...]
        for block, score, grad_chance, bias in zip(blocks, scores, grad_chances, biases):
            at = norm + bias
            parts = [
                (jnp.exp2(x * SCALE2 - at) * (y - delta)).astype(jnp.bfloat16)
                for x, y in zip(thirds(score), thirds(grad_chance))
            ]
            sum_of = sum_of + matmul(jnp.concatenate(parts, axis=1), kv[block, :ROWS], NN_DIMS)
        acc[...] = sum_of

    each_group(number, BACKWARD_GROUP, wait, step)
    out_ref[...] = acc[...].astype(out_ref.dtype)


def stat_rows(stat):
    for kind in range(2):
        pieces = []
        for row in range(9 * kind, 9 * kind + 3):
            pieces.append(stat[row : row + 1] + (stat[row + 3 : row + 4] + stat[row + 6 : row + 7]))
        yield jnp.concatenate(pieces, axis=1)


def key_side(
    flags, k_ref, v_ref, n0, l0, l1, l2, m0, m1, m2, n1, n2, key_out, value_out, qg, sems, key_acc, value_acc
):
    slots = []
    for near, line, columns in ((n0, l0, m0), (n1, l1, m1), (n2, l2, m2)):
        for w, rows in enumerate((line, columns.at[0], columns.at[1])):
            slots += [(near, w, rows, t) for t in range(3)]
    data = pl.ds(0, 2 * ROWS)

    def each_slot(act):
        place = jnp.int32(0)
        for at, (near, w, rows, t) in enumerate(slots):
            flag = flags[PLACES + at]
            pl.when(flag == 1)(lambda place=place, slot=(near, w, rows, t): act(place, *slot))
            place = place + flag
        return place

    def start(place, near, w, rows, t):
        if t == 0 and near is not n0:
            source = near.at[w, pl.ds(2 * ROWS, 2 * ROWS)]
            pltpu.make_async_copy(source, qg.at[place, data], sems.at[place]).start()

    def move(place, near, w, rows, t):
        if t > 0:
            qg[place] = rows[BLOCK_ROWS * (t - 1) : BLOCK_ROWS * t]
        else:
            qg[place, 2 * ROWS :] = rows[2 * BLOCK_ROWS :]
            if near is n0:
                qg[place, : 2 * ROWS] = near[w, 2 * ROWS :]

    def wait(place, near, w, rows, t):
        if t == 0 and near is not n0:
            pltpu.make_async_copy(qg.at[place, data], qg.at[place, data], sems.at[place]).wait()

    each_slot(start)
    number = each_slot(move)
    each_slot(wait)
    key_acc[...] = jnp.zeros(key_acc.shape, jnp.float32)
    value_acc[...] = jnp.zeros(value_acc.shape, jnp.float32)

    def step(blocks, biases):
        key, value = k_ref[...], v_ref[...]
        scores = [matmul(key, qg[b, :ROWS], NT_DIMS) for b in blocks]
        grad_chances = [matmul(value, qg[b, ROWS : 2 * ROWS], NT_DIMS) for b in blocks]
        key_sum, value_sum = key_acc[...], value_acc[...]
        for block, score, grad_chance, bias in zip(blocks, scores, grad_chances, biases):
            norm, delta = stat_rows(qg[block, 2 * ROWS :].astype(jnp.float32))
            chance = jnp.exp2(score * SCALE2 - (norm + bias))
            grad_score = (chance * (grad_chance - delta)).astype(jnp.bfloat16)
            value_sum = value_sum + matmul(chance.astype(jnp.bfloat16), qg[block, ROWS : 2 * ROWS], NN_DIMS)
            key_sum = key_sum + matmul(grad_score, qg[block, :ROWS], NN_DIMS)
        key_acc[...] = key_sum
        value_acc[...] = value_sum

    each_group(number, BACKWARD_GROUP, no_wait, step)
    key_out[...] = (key_acc[...] * SCALE).astype(key_out.dtype)
    value_out[...] = value_acc[...].astype(value_out.dtype)


def call(kernel, name, halo, out_shape, scratch):
    smem = pl.BlockSpec(memory_space=pltpu.SMEM)
    vmem = pl.BlockSpec(memory_space=pltpu.VMEM)
    anywhere = pl.BlockSpec(memory_space=pl.ANY)
    area = PLACES * ROWS * ROWS

    def run(*operands):
        return pl.pallas_call(
            kernel,
            out_shape=out_shape,
            in_specs=[smem]
            + [anywhere if i in halo else vmem for i in range(1, len(operands))],
            out_specs=jax.tree.map(lambda _: vmem, out_shape),
            scratch_shapes=scratch,
            compiler_params=pltpu.CompilerParams(vmem_limit_bytes=VMEM_LIMIT),
            cost_estimate=pl.CostEstimate(
                flops=area * DEPTH * 8, transcendentals=area, bytes_accessed=PLACES * ROWS * DEPTH * 4
            ),
            name=name,
        )(*operands)

    return run


def join(parts, *after):
    count = len(parts)
    starts = np.cumsum([0] + [x.shape[0] for x in parts])

    def kernel(*refs):
        out = refs[-1]
        for i in range(count):
            out[int(starts[i]) : int(starts[i + 1])] = refs[i][...]

    vmem = pl.BlockSpec(memory_space=pltpu.VMEM)
    anywhere = pl.BlockSpec(memory_space=pl.ANY)
    return pl.pallas_call(
        kernel,
        out_shape=jax.ShapeDtypeStruct((int(starts[-1]),) + parts[0].shape[1:], parts[0].dtype),
        in_specs=[vmem] * count + [anywhere] * len(after),
        out_specs=vmem,
        compiler_params=pltpu.CompilerParams(vmem_limit_bytes=JOIN_LIMIT),
        name="join",
    )(*parts, *after)


def last_two(own, *after):
    def kernel(*refs):
        refs[-1][...] = refs[0][:, 2:]

    vmem = pl.BlockSpec(memory_space=pltpu.VMEM)
    anywhere = pl.BlockSpec(memory_space=pl.ANY)
    return pl.pallas_call(
        kernel,
        out_shape=jax.ShapeDtypeStruct((1, 2, ROWS, DEPTH), own.dtype),
        in_specs=[vmem] + [anywhere] * len(after),
        out_specs=vmem,
        compiler_params=pltpu.CompilerParams(vmem_limit_bytes=JOIN_LIMIT),
        name="last_two",
    )(own, *after)


def kernels():
    wide = jax.ShapeDtypeStruct((ROWS, DEPTH), jnp.float32)
    narrow = jax.ShapeDtypeStruct((ROWS, DEPTH), jnp.bfloat16)
    stat_shape = jax.ShapeDtypeStruct((STAT_ROWS, DEPTH), jnp.bfloat16)
    stat_scratch = pltpu.VMEM((STAT_ROWS, DEPTH), jnp.float32)
    blocks = pltpu.VMEM((PLACES, 2 * ROWS, DEPTH), jnp.bfloat16)
    stat_blocks = pltpu.VMEM((PLACES, BLOCK_ROWS, DEPTH), jnp.bfloat16)
    sems = pltpu.SemaphoreType.DMA((PLACES,))
    wide_scratch = pltpu.VMEM((ROWS, DEPTH), jnp.float32)
    return (
        call(forward_near, "forward_near", range(3, 5), (wide, wide, wide), [blocks, sems]),
        call(
            forward_rest,
            "forward_rest",
            range(4, 6),
            (narrow, stat_shape, wide, wide),
            [blocks, sems] + [wide_scratch] * 3 + [stat_scratch],
        ),
        call(query_side, "query_side", range(7, 11), narrow, [blocks, sems, wide_scratch]),
        call(
            key_side,
            "key_side",
            range(10, 12),
            (narrow, narrow),
            [stat_blocks, sems] + [wide_scratch] * 2,
        ),
    )


def on_device(queries, keys, values, out_grad, window_extent, pair_table):
    out_block = queries.shape
    q, k, v, g = (x.reshape(ROWS, DEPTH) for x in (queries, keys, values, out_grad))
    flags = allowed_slots(window_extent, pair_table)
    run_near, run_rest, run_query, run_key = kernels()

    kv = jnp.stack([k, v])[None]
    kv_planes = swap(kv, "ta")
    own = join([kv[0], q[None], g[None]])[None]
    near_row = join([own] + swap(own, "wa"))
    near = [x.reshape(3, 4 * ROWS, DEPTH) for x in [near_row] + swap(near_row, "ha")]
    kv_middle = join(kv_planes)
    kv_row = join([kv_middle] + swap(kv_middle, "wa"))
    kv_rest = [x.reshape(6, 2 * ROWS, DEPTH) for x in [kv_row] + swap(kv_row, "ha")]
    qg_planes = swap(last_two(own, kv_row), "ta")
    state = run_near(flags, q, *near)
    attended, stat, norm, delta = run_rest(flags, q, g, *kv_rest, *state)
    pieces = []
    for plane, plane_stat in zip(qg_planes, swap(stat, "ta")):
        pieces += [plane.reshape(2 * ROWS, DEPTH), plane_stat]
    line = join(pieces + [stat])
    sides = swap(line, "wa")
    lines = [line] + swap(line, "ha")
    columns = join([x[None] for x in sides], *lines[1:])
    columns = [columns] + swap(columns, "ha")
    query_grad = run_query(
        flags, q, g, norm, delta, near[0], kv_rest[0], *near[1:], *kv_rest[1:]
    )
    key_grad, value_grad = run_key(flags, k, v, near[0], *lines, *columns, *near[1:])
    return tuple(x.reshape(out_block) for x in (attended, query_grad, key_grad, value_grad))


def solution(mesh):
    split = P("ta", "ha", "wa", None)
    return jax.shard_map(
        on_device,
        mesh=mesh,
        in_specs=(split, split, split, split, P(), P()),
        out_specs=(split, split, split, split),
        check_vma=False,
    )
```
